256 devices in a mesh: tm: 8 (over z), space: 32 (over y, x, core).
Axes of the slice: x: 4, y: 4, z: 8, core: 2. Of those that a mesh axis runs over, the one named last changes fastest.
Arguments:
- features: bfloat16 [16, 256, 80, 256], P('tm', 'space'), may hold values from -24 to 24
- conv_weights: bfloat16 [2, 3, 3, 3, 256, 256], replicated, may hold values from -0.078125 to 0.078125
- conv_bias: float32 [2, 256], replicated, may hold values from -3 to 3
- norm_gain: float32 [2, 256], replicated, may hold values from 0.1 to 1.9
- norm_shift: float32 [2, 256], replicated, may hold values from -3 to 3
Outputs:
- block_out: bfloat16 [16, 256, 80, 256], P('tm', 'space')
The draws below stay inside these ranges and needn't reach their ends.
All inputs are finite; a program needn't handle non-finite values.
Results may differ from the reference program's by a relative error of at most 0.008.
Values may be sent and summed in bfloat16 or wider, within the bound.
A program may use at most 64 MiB of HBM per device.

```python
import math
import jax
import jax.numpy as jnp
from jax import lax

C = 256
GROUPS = 32
FR_DEV = 2
ROWS_DEV = 8
W = 80
FRAMES = 16
HEIGHT = 256


def draw_features(key, part):
    key = jax.random.fold_in(key, 7)
    key_noise = jax.random.fold_in(key, 0)
    key_rough = jax.random.fold_in(key, 1)
    key_chan = jax.random.fold_in(key, 2)
    key_plane = jax.random.fold_in(key, 4)
    key_strip = jax.random.fold_in(key, 5)
    place = (jnp.arange(FRAMES)[:, None] * HEIGHT + jnp.arange(HEIGHT)[None, :]).astype(jnp.float32) / (FRAMES * HEIGHT)
    rough = jax.random.uniform(key_rough, (FRAMES, HEIGHT), minval=0.0, maxval=math.log(10.0))
    scales = 0.15 * jnp.exp(place * math.log(3.0) + rough)
    channel_scale = jnp.exp(jax.random.uniform(key_chan, (C,), minval=-0.5, maxval=0.5))
    plane_table = jax.random.uniform(key_plane, (FRAMES // FR_DEV, C), minval=-1.0, maxval=1.0)
    strip_table = jax.random.uniform(key_strip, (HEIGHT // ROWS_DEV, C), minval=-1.0, maxval=1.0)
    plane_offset = jnp.repeat(plane_table, FR_DEV, axis=0)
    strip_offset = jnp.repeat(strip_table, ROWS_DEV, axis=0)
    region = plane_offset[:, None, :] + strip_offset[None, :, :]
    noise = jax.random.normal(key_noise, (FRAMES, HEIGHT, W, C))
    values = (noise * scales[:, :, None, None] + region[:, :, None, :]) * channel_scale
    return jnp.clip(values, -24.0, 24.0).astype(jnp.bfloat16)


def bell_draw(key, dims, scale, reach, held_as=jnp.bfloat16):
    return jnp.clip(scale * jax.random.normal(key, dims, jnp.float32), -reach, reach).astype(held_as)


def setup_inputs(seed: int = 0) -> dict:
    arg_keys = jax.random.split(jax.random.key(seed), 6)
    features = draw_features(jax.random.fold_in(arg_keys[5], 71), 0)
    conv_weights = bell_draw(arg_keys[1], (2, 3, 3, 3, C, C), (27 * C) ** -0.5, 0.078125)
    conv_bias = bell_draw(arg_keys[2], (2, C), 0.5, 3.0, jnp.float32)
    norm_gain = jnp.clip(1.0 + 0.18 * jax.random.normal(arg_keys[3], (2, C), jnp.float32), 0.1, 1.9)
    norm_shift = bell_draw(arg_keys[4], (2, C), 0.5, 3.0, jnp.float32)
    return dict(features=features, conv_weights=conv_weights, conv_bias=conv_bias, norm_gain=norm_gain, norm_shift=norm_shift)


def group_norm(field, gain, shift):
    grouped = field.reshape(FRAMES, HEIGHT, W, GROUPS, C // GROUPS)
    average = lax.optimization_barrier(jnp.mean(grouped, axis=(0, 1, 2, 4)))
    centered = grouped - average[:, None]
    variance = lax.optimization_barrier(jnp.mean(centered * centered, axis=(0, 1, 2, 4)))
    normed = centered / jnp.sqrt(variance + 1e-06)[:, None]
    normed = normed.reshape(FRAMES, HEIGHT, W, C) * gain + shift
    return jax.nn.silu(normed).astype(jnp.bfloat16)

def causal_conv(field, weights, bias):
    padded = jnp.concatenate([field[:1], field[:1], field], 0)
    padded = jnp.pad(padded, ((0, 0), (1, 1), (1, 1), (0, 0)))

    def one_frame(index):
        window = lax.dynamic_slice_in_dim(padded, index, 3, 0)
        total = jnp.zeros((HEIGHT * W, C), jnp.float32)
        for offset_t in range(3):
            for offset_h in range(3):
                patch = jnp.concatenate([window[offset_t, offset_h:offset_h + HEIGHT, shift_w:shift_w + W] for shift_w in range(3)], -1)
                total = total + jnp.dot(patch.reshape(HEIGHT * W, 3 * C), weights[offset_t, offset_h].reshape(3 * C, C), preferred_element_type=jnp.float32)
        return total.reshape(HEIGHT, W, C)
    return lax.map(one_frame, jnp.arange(FRAMES, dtype=jnp.int32)) + bias

def reference(features, conv_weights, conv_bias, norm_gain, norm_shift):
    first = group_norm(features.astype(jnp.float32), norm_gain[0], norm_shift[0])
    middle = causal_conv(first, conv_weights[0], conv_bias[0]).astype(jnp.bfloat16)
    second = group_norm(middle.astype(jnp.float32), norm_gain[1], norm_shift[1])
    result = features.astype(jnp.float32) + causal_conv(second, conv_weights[1], conv_bias[1])
    return result.astype(jnp.bfloat16)
```

```python
import functools

import jax
import jax.numpy as jnp
from jax import lax
from jax.experimental import pallas as pl
from jax.experimental.pallas import tpu as pltpu
from jax.sharding import PartitionSpec as P

GROUP = 8
EPS = 1e-06
DMA = pltpu.SemaphoreType.DMA

HALO_0 = ((0, 1), (7, 1), (1, 2), (3, 2), (5, 2))
HALO_1 = ((0, 1), (1, 3), (7, 1), (4, 1), (5, 2))
STEPS_0 = ((0, 2, (2,)), (2, 2, (3,)), (4, 4, (4,)))
STEPS_1 = ((0, 2, (1,)), (2, 2, (3,)), (4, 4, (4,)))


def lane_groups(tile):
    lanes = tile.shape[1]
    lane = lax.broadcasted_iota(jnp.int32, tile.shape, 1)
    step = 1
    while step < GROUP:
        ahead = pltpu.roll(tile, lanes - step, 1)
        behind = pltpu.roll(tile, step, 1)
        tile = tile + jnp.where(lane % (2 * step) < step, ahead, behind)
        step *= 2
    return tile


def merged(parts, each):
    total = jnp.sum(parts, 0)
    mean = total * (1.0 / parts.shape[0])
    off = parts - mean
    spread = jnp.sum(off * off, 0) * each
    shifted = pltpu.roll(spread, 2, 0)
    line = lax.broadcasted_iota(jnp.int32, total.shape, 0)
    return jnp.where(line < 2, mean, total + shifted)


def packed(mean, squares):
    half = mean.shape[1] // 2
    line = lax.broadcasted_iota(jnp.int32, (8, half), 0)
    rows = (mean[:, :half], mean[:, half:], squares[:, :half], squares[:, half:])
    tile = jnp.zeros((8, half), jnp.float32)
    for i, row in enumerate(rows):
        tile = jnp.where(line == i, jnp.broadcast_to(row, (8, half)), tile)
    return tile


def affine(tile, count, gain, shift):
    mean = lane_groups(tile) * (1.0 / GROUP)
    off = tile - mean
    inner = pltpu.roll(off * off * count, 2, 0)
    variance = lane_groups(tile + inner) * (1.0 / (GROUP * count))
    mean = jnp.concatenate([mean[0:1], mean[1:2]], 1)
    variance = jnp.concatenate([variance[2:3], variance[3:4]], 1)
    return mean, gain / jnp.sqrt(variance + EPS), shift


def activated(raw, norm):
    mean, scale, shift = norm
    u = (raw.astype(jnp.float32) - mean) * scale + shift
    return u / (1.0 + jnp.exp(-u))


def folded(value):
    cells, chans = value.shape
    return jnp.sum(value.reshape(cells // 8, 8, chans), 0)


def joined(wide, rows, columns, chans):
    wide = wide.reshape(rows, columns, 3 * chans)
    column = lax.broadcasted_iota(jnp.int32, (rows, columns, chans), 1)
    left = jnp.where(column == 0, 0.0, pltpu.roll(wide[:, :, :chans], 1, 1))
    right = jnp.where(
        column == columns - 1, 0.0, pltpu.roll(wide[:, :, 2 * chans :], columns - 1, 1)
    )
    return left + wide[:, :, chans : 2 * chans] + right


def products(field, weight, layer, taps, row, rows):
    columns, chans = field.shape[2:]
    left = [
        field[frame, row + dh : row + dh + rows].reshape(rows * columns, chans)
        for _, frame in taps
        for dh in range(3)
    ]
    right = [weight[layer, dt].reshape(3 * chans, 3 * chans) for dt, _ in taps]
    wide = jnp.dot(
        jnp.concatenate(left, 1),
        jnp.concatenate(right, 0),
        preferred_element_type=jnp.float32,
    )
    return joined(wide, rows, columns, chans)


def kernel(
    frames_all, lines_all,
    features, weights, bias, gain, shift, out,
    raw0, raw1, act0, act1, weight, total, result, space_stats, tm_stats, pivot,
    in_sem, weight_sem, out_sem,
    halo_send, halo_recv, edge_send, edge_recv, far_send, far_recv, stat_send, stat_recv,
):
    t, s = lax.axis_index("tm"), lax.axis_index("space")
    later, above, below = lax.rem(t + 1, frames_all), lax.rem(s + lines_all - 1, lines_all), lax.rem(s + 1, lines_all)
    frames, rows, columns, chans = result.shape
    cells = frames * rows * columns
    first = t == 0
    raws, acts = (raw0, raw1), (act0, act1)

    load = pltpu.make_async_copy(features, raw0.at[pl.ds(2, frames), pl.ds(1, rows)], in_sem)
    load.start()
    loads = []
    for layer in range(2):
        for dw in range(3):
            loads.append(
                pltpu.make_async_copy(
                    weights.at[layer, :, :, dw],
                    weight.at[layer, :, :, :, pl.ds(dw * chans, chans)],
                    weight_sem.at[layer, dw],
                )
            )
            loads[-1].start()

    barrier = pltpu.get_barrier_semaphore()

    @pl.loop(1, lines_all)
    def _(j):
        pl.semaphore_signal(barrier, inc=1, device_id=(t, lax.rem(s + j, lines_all)), device_id_type=pl.DeviceIdType.MESH)

    @pl.loop(1, frames_all)
    def _(j):
        pl.semaphore_signal(barrier, inc=1, device_id=(lax.rem(t + j, frames_all), s), device_id_type=pl.DeviceIdType.MESH)

    def remote(source, target, send, recv, device):
        return pltpu.make_async_remote_copy(
            src_ref=source, dst_ref=target, send_sem=send, recv_sem=recv,
            device_id=device, device_id_type=pl.DeviceIdType.MESH,
        )

    def halo(layer, order, k):
        row, count = order[k]
        raw = raws[layer]
        return remote(
            raw.at[pl.ds(2, 2), pl.ds(1 + row, count)],
            raw.at[pl.ds(0, 2), pl.ds(1 + row, count)],
            halo_send.at[layer, k], halo_recv.at[layer, k], (later, s),
        )

    def edge(layer, frame, side, sems):
        raw = raws[layer]
        source, target = ((1, rows + 1), (rows, 0))[side]
        return remote(
            raw.at[pl.ds(frame, 2), source], raw.at[pl.ds(frame, 2), target],
            sems[0].at[layer, side], sems[1].at[layer, side], (t, (above, below)[side]),
        )

    def own_edge(layer, side):
        return edge(layer, 2, side, (edge_send, edge_recv))

    def far_edge(layer, side):
        return edge(layer, 0, side, (far_send, far_recv))

    def spread_start(layer, stage):
        buffer = (space_stats, tm_stats)[stage]
        number = buffer.shape[1]

        @pl.loop(1, number)
        def _(j):
            device = ((t, lax.rem(s + j, lines_all)), (lax.rem(t + j, frames_all), s))[stage]
            remote(
                buffer.at[layer, 0], buffer.at[layer, j],
                stat_send.at[layer, stage], stat_recv.at[layer, stage], device,
            ).start()

    def spread_wait(layer, stage, sems):
        buffer = (space_stats, tm_stats)[stage]
        rest = buffer.at[layer, pl.ds(1, buffer.shape[1] - 1)]
        pltpu.make_async_copy(rest, rest, sems.at[layer, stage]).wait()

    def normalize(layer, norm, frame, row, count):
        raw, act = raws[layer], acts[layer]
        value = raw[frame, pl.ds(row, count)]
        if isinstance(frame, int) and frame < 2:
            value = jnp.where(first, raw[2, pl.ds(row, count)], value)
        value = activated(value, norm)
        if isinstance(row, int) and row in (0, rows + 1):
            outside = s == (0 if row == 0 else lines_all - 1)
            value = jnp.where(outside, 0.0, value)
        act[frame, pl.ds(row, count)] = value.astype(jnp.bfloat16)

    def own_part(layer, norm):
        for side in range(2):
            own_edge(layer, side).wait_recv()
        for frame in (2, 3):
            for row in (0, rows + 1):
                normalize(layer, norm, frame, row, 1)

            @pl.loop(0, rows)
            def _(row):
                normalize(layer, norm, frame, row + 1, 1)

        if layer == 0:
            for dw in range(3):
                loads[dw].wait()
        else:
            for dw in range(3):
                loads[3 + dw].wait()
        act = acts[layer]
        total[0] = products(act, weight, layer, ((2, 2),), 0, rows) + bias[layer : layer + 1]
        total[1] = products(act, weight, layer, ((1, 2), (2, 3)), 0, rows) + bias[layer : layer + 1]

    def halo_part(layer, norm, steps, order, finish):
        act = acts[layer]
        done = 0
        ready = -1
        for k, (row, count, need) in enumerate(steps):
            for c in range(done, need[-1] + 1):
                if order[c][0] not in (0, rows - 1):
                    halo(layer, order, c).wait_recv()
            done = need[-1] + 1
            if k == 0:
                far_edge(layer, 1).wait_recv()
                for frame in (0, 1):
                    normalize(layer, norm, frame, 0, 1)
            if k == len(steps) - 1:
                far_edge(layer, 0).wait_recv()
                for frame in (0, 1):
                    normalize(layer, norm, frame, rows + 1, 1)
            upto = min(row + count, rows - 1)
            for frame in (0, 1):
                normalize(layer, norm, frame, ready + 2, upto - ready)
            ready = upto
            values = (
                products(act, weight, layer, ((0, 0), (1, 1)), row, count),
                products(act, weight, layer, ((0, 1),), row, count),
            )
            finish(k, row, count, values)

    load.wait()

    def lines(f):
        return lax.fori_loop(
            0, frames * rows,
            lambda i, carry: carry + folded(f(raw0[2 + i // rows, 1 + i % rows].astype(jnp.float32))),
            jnp.zeros((8, chans), jnp.float32),
        )

    mean = jnp.sum(lines(lambda v: v), 0, keepdims=True) * (1.0 / cells)
    squares = jnp.sum(lines(lambda v: (v - mean) * (v - mean)), 0, keepdims=True)
    space_stats[0, 0] = packed(mean, squares)

    pl.semaphore_wait(barrier, lines_all + frames_all - 2)

    halo(0, HALO_0, 0).start()
    halo(0, HALO_0, 1).start()
    spread_start(0, 0)
    for side in range(2):
        own_edge(0, side).start()
    for k in range(2, len(HALO_0)):
        halo(0, HALO_0, k).start()

    def statistics(layer, order, between):
        spread_wait(layer, 0, stat_recv)
        tm_stats[layer, 0] = merged(space_stats[layer], float(cells))
        spread_start(layer, 1)
        between()
        spread_wait(layer, 1, stat_recv)
        tile = merged(tm_stats[layer], float(cells * lines_all))
        return affine(
            tile, float(cells * lines_all * frames_all),
            gain[layer : layer + 1], shift[layer : layer + 1],
        )

    def forward_edges(layer, order):
        for k, (row, _) in enumerate(order):
            if row in (0, rows - 1):
                halo(layer, order, k).wait_recv()
                far_edge(layer, 0 if row == 0 else 1).start()

    norm0 = statistics(0, HALO_0, lambda: forward_edges(0, HALO_0))
    own_part(0, norm0)

    sums = [jnp.zeros((8, chans), jnp.float32), jnp.zeros((8, chans), jnp.float32)]

    def finish_0(k, row, count, values):
        chunk = []
        for frame in range(2):
            value = (total[frame, row : row + count] + values[frame]).astype(jnp.bfloat16)
            raw1[2 + frame, 1 + row : 1 + row + count] = value
            chunk.append(value.astype(jnp.float32).reshape(count * columns, chans))
        if k == 0:
            pivot[...] = jnp.sum(folded(chunk[0]) + folded(chunk[1]), 0, keepdims=True) * (
                1.0 / (2 * count * columns)
            )
        base = pivot[...]
        for value in chunk:
            off = value - base
            sums[0] = sums[0] + folded(off)
            sums[1] = sums[1] + folded(off * off)
        if k == 0:
            own_edge(1, 0).start()
        if k == len(STEPS_0) - 2:
            for c in range(len(HALO_0)):
                halo(0, HALO_0, c).wait_send()
            halo(1, HALO_1, 0).start()
            halo(1, HALO_1, 1).start()
        if k == len(STEPS_0) - 1:
            own_edge(1, 1).start()
            for c in range(2, len(HALO_1)):
                halo(1, HALO_1, c).start()

    halo_part(0, norm0, STEPS_0, HALO_0, finish_0)

    off_mean = jnp.sum(sums[0], 0, keepdims=True) * (1.0 / cells)
    off_squares = jnp.sum(sums[1], 0, keepdims=True)
    space_stats[1, 0] = packed(pivot[...] + off_mean, off_squares - off_mean * off_mean * cells)
    spread_start(1, 0)
    norm1 = statistics(1, HALO_1, lambda: forward_edges(1, HALO_1))
    own_part(1, norm1)

    def store(k, row, count):
        return pltpu.make_async_copy(
            result.at[:, pl.ds(row, count)], out.at[:, pl.ds(row, count)], out_sem.at[k]
        )

    def finish_1(k, row, count, values):
        for frame in range(2):
            value = total[frame, row : row + count] + values[frame]
            value = value + raw0[2 + frame, 1 + row : 1 + row + count].astype(jnp.float32)
            result[frame, row : row + count] = value.astype(jnp.bfloat16)
        store(k, row, count).start()

    halo_part(1, norm1, STEPS_1, HALO_1, finish_1)

    for layer in range(2):
        for stage in range(2):
            spread_wait(layer, stage, stat_send)
        for side in range(2):
            own_edge(layer, side).wait_send()
            far_edge(layer, side).wait_send()
    for k in range(len(HALO_1)):
        halo(1, HALO_1, k).wait_send()
    for k, (row, count, _) in enumerate(STEPS_1):
        store(k, row, count).wait()


def shards(features, weights, bias, gain, shift):
    frames, rows, columns, chans = features.shape
    frames_all, lines_all = lax.axis_size("tm"), lax.axis_size("space")
    field = pltpu.VMEM((frames + 2, rows + 2, columns, chans), jnp.bfloat16)
    anywhere, here = pl.BlockSpec(memory_space=pl.ANY), pl.BlockSpec(memory_space=pltpu.VMEM)
    return pl.pallas_call(
        functools.partial(kernel, frames_all, lines_all),
        out_shape=jax.ShapeDtypeStruct(features.shape, features.dtype),
        in_specs=[anywhere, anywhere, here, here, here],
        out_specs=anywhere,
        scratch_shapes=[
            field, field, field, field,
            pltpu.VMEM((2, 3, 3, chans, 3 * chans), jnp.bfloat16),
            pltpu.VMEM((frames, rows, columns, chans), jnp.float32),
            pltpu.VMEM((frames, rows, columns, chans), jnp.bfloat16),
            pltpu.VMEM((2, lines_all, 8, 128), jnp.float32),
            pltpu.VMEM((2, frames_all, 8, 128), jnp.float32),
            pltpu.VMEM((1, chans), jnp.float32),
            DMA, DMA((2, 3)), DMA((len(STEPS_1),)),
            DMA((2, len(HALO_0))), DMA((2, len(HALO_0))),
            DMA((2, 2)), DMA((2, 2)), DMA((2, 2)), DMA((2, 2)),
            DMA((2, 2)), DMA((2, 2)),
        ],
        compiler_params=pltpu.CompilerParams(
            collective_id=0, has_side_effects=True, vmem_limit_bytes=56 * 2**20
        ),
        cost_estimate=pl.CostEstimate(
            flops=4 * frames * rows * columns * 27 * chans * chans,
            bytes_accessed=2 * features.size * 2 + weights.size * 2,
            transcendentals=0,
        ),
    )(features, weights, bias, gain, shift)


def solution(mesh):
    placed = (P("tm", "space", None, None), P(), P(), P(), P())
    return jax.shard_map(
        shards, mesh=mesh, in_specs=placed, out_specs=P("tm", "space", None, None), check_vma=False
    )
```

```python
import functools

import jax
import jax.numpy as jnp
from jax import lax
from jax.experimental import pallas as pl
from jax.experimental.pallas import tpu as pltpu
from jax.sharding import PartitionSpec as P

GROUP = 8
EPS = 1e-06
DMA = pltpu.SemaphoreType.DMA

HALO_0 = ((0, 1), (7, 1), (1, 1), (2, 1), (3, 2), (5, 2))
HALO_1 = ((0, 1), (1, 3), (7, 1), (4, 1), (5, 2))
AHEAD = (3, 2)
STEPS_0 = ((0, 2, 3), (2, 2, 4), (4, 4, 5))
STEPS_1 = ((0, 2, 1), (2, 2, 3), (4, 4, 4))


def lane_groups(tile):
    lanes = tile.shape[1]
    lane = lax.broadcasted_iota(jnp.int32, tile.shape, 1)
    step = 1
    while step < GROUP:
        ahead = pltpu.roll(tile, lanes - step, 1)
        behind = pltpu.roll(tile, step, 1)
        tile = tile + jnp.where(lane % (2 * step) < step, ahead, behind)
        step *= 2
    return tile


def merged(parts, each):
    total = jnp.sum(parts, 0)
    mean = total * (1.0 / parts.shape[0])
    off = parts - mean
    spread = jnp.sum(off * off, 0) * each
    shifted = pltpu.roll(spread, 2, 0)
    line = lax.broadcasted_iota(jnp.int32, total.shape, 0)
    return jnp.where(line < 2, mean, total + shifted)


def packed(mean, squares):
    half = mean.shape[1] // 2
    line = lax.broadcasted_iota(jnp.int32, (8, half), 0)
    rows = (mean[:, :half], mean[:, half:], squares[:, :half], squares[:, half:])
    tile = jnp.zeros((8, half), jnp.float32)
    for i, row in enumerate(rows):
        tile = jnp.where(line == i, jnp.broadcast_to(row, (8, half)), tile)
    return tile


def affine(tile, count, gain, shift):
    mean = lane_groups(tile) * (1.0 / GROUP)
    off = tile - mean
    inner = pltpu.roll(off * off * count, 2, 0)
    variance = lane_groups(tile + inner) * (1.0 / (GROUP * count))
    mean = jnp.concatenate([mean[0:1], mean[1:2]], 1)
    variance = jnp.concatenate([variance[2:3], variance[3:4]], 1)
    return mean, gain / jnp.sqrt(variance + EPS), shift


def activated(raw, norm):
    mean, scale, shift = norm
    u = (raw.astype(jnp.float32) - mean) * scale + shift
    return u / (1.0 + jnp.exp(-u))


def folded(value):
    cells, chans = value.shape
    return jnp.sum(value.reshape(cells // 8, 8, chans), 0)


def joined(wide, rows, columns, chans):
    wide = wide.reshape(rows, columns, 3 * chans)
    column = lax.broadcasted_iota(jnp.int32, (rows, columns, chans), 1)
    left = jnp.where(column == 0, 0.0, pltpu.roll(wide[:, :, :chans], 1, 1))
    right = jnp.where(
        column == columns - 1, 0.0, pltpu.roll(wide[:, :, 2 * chans :], columns - 1, 1)
    )
    return left + wide[:, :, chans : 2 * chans] + right


def products(field, weight, layer, taps, row, rows):
    columns, chans = field.shape[2:]
    left = [
        field[frame, row + dh : row + dh + rows].reshape(rows * columns, chans)
        for _, frame in taps
        for dh in range(3)
    ]
    right = [weight[layer, dt].reshape(3 * chans, 3 * chans) for dt, _ in taps]
    wide = jnp.dot(
        jnp.concatenate(left, 1),
        jnp.concatenate(right, 0),
        preferred_element_type=jnp.float32,
    )
    return joined(wide, rows, columns, chans)


def kernel(
    frames_all, lines_all,
    features, weights, bias, gain, shift, out,
    raw0, raw1, act0, act1, weight, total, space_stats, tm_stats, pivot,
    in_sem, weight_sem,
    halo_send, halo_recv, edge_send, edge_recv, far_send, far_recv, stat_send, stat_recv,
):
    t, s = lax.axis_index("tm"), lax.axis_index("space")
    later, above, below = lax.rem(t + 1, frames_all), lax.rem(s + lines_all - 1, lines_all), lax.rem(s + 1, lines_all)
    frames, rows, columns, chans = out.shape
    cells = frames * rows * columns
    first = t == 0
    raws, acts = (raw0, raw1), (act0, act1)

    barrier = pltpu.get_barrier_semaphore()

    @pl.loop(1, lines_all)
    def _(j):
        pl.semaphore_signal(barrier, inc=1, device_id=(t, lax.rem(s + j, lines_all)), device_id_type=pl.DeviceIdType.MESH)

    @pl.loop(1, frames_all)
    def _(j):
        pl.semaphore_signal(barrier, inc=1, device_id=(lax.rem(t + j, frames_all), s), device_id_type=pl.DeviceIdType.MESH)

    load = pltpu.make_async_copy(features, raw0.at[pl.ds(2, frames), pl.ds(1, rows)], in_sem)
    load.start()
    loads = []
    for layer in range(2):
        for dw in range(3):
            loads.append(
                pltpu.make_async_copy(
                    weights.at[layer, :, :, dw],
                    weight.at[layer, :, :, :, pl.ds(dw * chans, chans)],
                    weight_sem.at[layer, dw],
                )
            )
            loads[-1].start()

    def remote(source, target, send, recv, device):
        return pltpu.make_async_remote_copy(
            src_ref=source, dst_ref=target, send_sem=send, recv_sem=recv,
            device_id=device, device_id_type=pl.DeviceIdType.MESH,
        )

    def halo(layer, order, k):
        row, count = order[k]
        raw = raws[layer]
        return remote(
            raw.at[pl.ds(2, 2), pl.ds(1 + row, count)],
            raw.at[pl.ds(0, 2), pl.ds(1 + row, count)],
            halo_send.at[layer, k], halo_recv.at[layer, k], (later, s),
        )

    def edge(layer, frame, side, sems):
        raw = raws[layer]
        source, target = ((1, rows + 1), (rows, 0))[side]
        return remote(
            raw.at[pl.ds(frame, 2), source], raw.at[pl.ds(frame, 2), target],
            sems[0].at[layer, side], sems[1].at[layer, side], (t, (above, below)[side]),
        )

    def own_edge(layer, side):
        return edge(layer, 2, side, (edge_send, edge_recv))

    def far_edge(layer, side):
        return edge(layer, 0, side, (far_send, far_recv))

    def spread_start(layer, stage):
        buffer = (space_stats, tm_stats)[stage]
        number = buffer.shape[1]

        @pl.loop(0, number - 1)
        def _(i):
            j = lax.rem(i + number // 3, number - 1) + 1
            device = ((t, lax.rem(s + j, lines_all)), (lax.rem(t + j, frames_all), s))[stage]
            remote(
                buffer.at[layer, 0], buffer.at[layer, j],
                stat_send.at[layer, stage], stat_recv.at[layer, stage], device,
            ).start()

    def spread_wait(layer, stage, sems):
        buffer = (space_stats, tm_stats)[stage]
        rest = buffer.at[layer, pl.ds(1, buffer.shape[1] - 1)]
        pltpu.make_async_copy(rest, rest, sems.at[layer, stage]).wait()

    def normalize(layer, norm, frame, row, count):
        raw, act = raws[layer], acts[layer]
        value = raw[frame, pl.ds(row, count)]
        if isinstance(frame, int) and frame < 2:
            value = jnp.where(first, raw[2, pl.ds(row, count)], value)
        value = activated(value, norm)
        if isinstance(row, int) and row in (0, rows + 1):
            outside = s == (0 if row == 0 else lines_all - 1)
            value = jnp.where(outside, 0.0, value)
        act[frame, pl.ds(row, count)] = value.astype(jnp.bfloat16)

    def own_part(layer, norm):
        for side in range(2):
            own_edge(layer, side).wait_recv()
        for frame in (2, 3):
            for row in (0, rows + 1):
                normalize(layer, norm, frame, row, 1)

            @pl.loop(0, rows)
            def _(row):
                normalize(layer, norm, frame, row + 1, 1)

        if layer == 0:
            for dw in range(3):
                loads[dw].wait()
        else:
            for dw in range(3):
                loads[3 + dw].wait()
        act = acts[layer]
        total[0] = products(act, weight, layer, ((2, 2),), 0, rows) + bias[layer : layer + 1]
        total[1] = products(act, weight, layer, ((1, 2), (2, 3)), 0, rows) + bias[layer : layer + 1]

    def halo_part(layer, norm, steps, order, finish):
        act = acts[layer]
        done = 0
        ready = -1
        for k, (row, count, need) in enumerate(steps):
            for c in range(done, need + 1):
                if order[c][0] not in (0, rows - 1):
                    halo(layer, order, c).wait_recv()
            done = need + 1
            if k == 0:
                far_edge(layer, 1).wait_recv()
                for frame in (0, 1):
                    normalize(layer, norm, frame, 0, 1)
            if k == len(steps) - 1:
                far_edge(layer, 0).wait_recv()
                for frame in (0, 1):
                    normalize(layer, norm, frame, rows + 1, 1)
            upto = min(row + count, rows - 1)
            for frame in (0, 1):
                normalize(layer, norm, frame, ready + 2, upto - ready)
            ready = upto
            values = (
                products(act, weight, layer, ((0, 0), (1, 1)), row, count),
                products(act, weight, layer, ((0, 1),), row, count),
            )
            finish(k, row, count, values)

    load.wait()

    def lines(f):
        return lax.fori_loop(
            0, frames * rows,
            lambda i, carry: carry + folded(f(raw0[2 + i // rows, 1 + i % rows].astype(jnp.float32))),
            jnp.zeros((8, chans), jnp.float32),
        )

    mean = jnp.sum(lines(lambda v: v), 0, keepdims=True) * (1.0 / cells)
    squares = jnp.sum(lines(lambda v: (v - mean) * (v - mean)), 0, keepdims=True)
    space_stats[0, 0] = packed(mean, squares)

    pl.semaphore_wait(barrier, lines_all + frames_all - 2)

    for k in range(AHEAD[0]):
        halo(0, HALO_0, k).start()
    spread_start(0, 0)
    for side in range(2):
        own_edge(0, side).start()

    def statistics(layer, order, between):
        spread_wait(layer, 0, stat_recv)
        tm_stats[layer, 0] = merged(space_stats[layer], float(cells))
        spread_start(layer, 1)
        for k in range(AHEAD[layer], len(order)):
            halo(layer, order, k).start()
        between()
        spread_wait(layer, 1, stat_recv)
        tile = merged(tm_stats[layer], float(cells * lines_all))
        return affine(
            tile, float(cells * lines_all * frames_all),
            gain[layer : layer + 1], shift[layer : layer + 1],
        )

    def forward_edges(layer, order):
        for k, (row, _) in enumerate(order):
            if row in (0, rows - 1):
                halo(layer, order, k).wait_recv()
                far_edge(layer, 0 if row == 0 else 1).start()

    norm0 = statistics(0, HALO_0, lambda: forward_edges(0, HALO_0))
    own_part(0, norm0)

    sums = [jnp.zeros((8, chans), jnp.float32), jnp.zeros((8, chans), jnp.float32)]

    def finish_0(k, row, count, values):
        chunk = []
        for frame in range(2):
            value = (total[frame, row : row + count] + values[frame]).astype(jnp.bfloat16)
            raw1[2 + frame, 1 + row : 1 + row + count] = value
            chunk.append(value.astype(jnp.float32).reshape(count * columns, chans))
        if k == 0:
            pivot[...] = jnp.sum(folded(chunk[0]) + folded(chunk[1]), 0, keepdims=True) * (
                1.0 / (2 * count * columns)
            )
        base = pivot[...]
        for value in chunk:
            off = value - base
            sums[0] = sums[0] + folded(off)
            sums[1] = sums[1] + folded(off * off)
        if k == 0:
            own_edge(1, 0).start()
        if k == len(STEPS_0) - 2:
            for c in range(AHEAD[1]):
                halo(1, HALO_1, c).start()

    halo_part(0, norm0, STEPS_0, HALO_0, finish_0)

    off_mean = jnp.sum(sums[0], 0, keepdims=True) * (1.0 / cells)
    off_squares = jnp.sum(sums[1], 0, keepdims=True)
    space_stats[1, 0] = packed(pivot[...] + off_mean, off_squares - off_mean * off_mean * cells)
    spread_start(1, 0)
    own_edge(1, 1).start()
    norm1 = statistics(1, HALO_1, lambda: forward_edges(1, HALO_1))
    own_part(1, norm1)

    def finish_1(k, row, count, values):
        for frame in range(2):
            value = total[frame, row : row + count] + values[frame]
            value = value + raw0[2 + frame, 1 + row : 1 + row + count].astype(jnp.float32)
            out[frame, row : row + count] = value.astype(jnp.bfloat16)

    halo_part(1, norm1, STEPS_1, HALO_1, finish_1)

    for layer in range(2):
        for stage in range(2):
            spread_wait(layer, stage, stat_send)
        for side in range(2):
            own_edge(layer, side).wait_send()
            far_edge(layer, side).wait_send()
    for k in range(len(HALO_0)):
        halo(0, HALO_0, k).wait_send()
    for k in range(len(HALO_1)):
        halo(1, HALO_1, k).wait_send()


def shards(features, weights, bias, gain, shift):
    frames, rows, columns, chans = features.shape
    frames_all, lines_all = lax.axis_size("tm"), lax.axis_size("space")
    field = pltpu.VMEM((frames + 2, rows + 2, columns, chans), jnp.bfloat16)
    there, here = pl.BlockSpec(memory_space=pltpu.HBM), pl.BlockSpec(memory_space=pltpu.VMEM)
    return pl.pallas_call(
        functools.partial(kernel, frames_all, lines_all),
        out_shape=pltpu.VMEM(features.shape, features.dtype),
        in_specs=[there, there, here, here, here],
        out_specs=here,
        scratch_shapes=[
            field, field, field, field,
            pltpu.VMEM((2, 3, 3, chans, 3 * chans), jnp.bfloat16),
            pltpu.VMEM((frames, rows, columns, chans), jnp.float32),
            pltpu.VMEM((2, lines_all, 8, 128), jnp.float32),
            pltpu.VMEM((2, frames_all, 8, 128), jnp.float32),
            pltpu.VMEM((1, chans), jnp.float32),
            DMA, DMA((2, 3)),
            DMA((2, 8)), DMA((2, 8)),
            DMA((2, 2)), DMA((2, 2)), DMA((2, 2)), DMA((2, 2)),
            DMA((2, 2)), DMA((2, 2)),
        ],
        compiler_params=pltpu.CompilerParams(
            collective_id=0, has_side_effects=True, vmem_limit_bytes=56 * 2**20
        ),
        cost_estimate=pl.CostEstimate(
            flops=4 * frames * rows * columns * 27 * chans * chans,
            bytes_accessed=2 * features.size * 2 + weights.size * 2,
            transcendentals=0,
        ),
    )(features, weights, bias, gain, shift)


def solution(mesh):
    placed = (P("tm", "space", None, None), P(), P(), P(), P())
    return jax.shard_map(
        shards, mesh=mesh, in_specs=placed, out_specs=P("tm", "space", None, None), check_vma=False
    )
```

```python
import functools

import jax
import jax.numpy as jnp
from jax import lax
from jax.experimental import pallas as pl
from jax.experimental.pallas import tpu as pltpu
from jax.sharding import PartitionSpec as P

GROUP = 8
EPS = 1e-06
DMA = pltpu.SemaphoreType.DMA

HALO_0 = ((0, 1), (7, 1), (1, 1), (2, 2), (4, 2), (6, 1))
HALO_1 = ((0, 1), (1, 2), (3, 1), (4, 1), (7, 1), (5, 1), (6, 1))
AHEAD = (3, 3)
STEPS_0 = ((0, 3, 3), (3, 2, 4), (5, 3, 5))
STEPS_1 = ((0, 3, 2), (3, 2, 5), (5, 3, 6))


def lane_groups(tile):
    lanes = tile.shape[1]
    lane = lax.broadcasted_iota(jnp.int32, tile.shape, 1)
    step = 1
    while step < GROUP:
        ahead = pltpu.roll(tile, lanes - step, 1)
        behind = pltpu.roll(tile, step, 1)
        tile = tile + jnp.where(lane % (2 * step) < step, ahead, behind)
        step *= 2
    return tile


def merged(parts, each):
    total = jnp.sum(parts, 0)
    mean = total * (1.0 / parts.shape[0])
    off = parts - mean
    spread = jnp.sum(off * off, 0) * each
    shifted = pltpu.roll(spread, 2, 0)
    line = lax.broadcasted_iota(jnp.int32, total.shape, 0)
    return jnp.where(line < 2, mean, total + shifted)


def packed(mean, squares):
    half = mean.shape[1] // 2
    line = lax.broadcasted_iota(jnp.int32, (8, half), 0)
    rows = (mean[:, :half], mean[:, half:], squares[:, :half], squares[:, half:])
    tile = jnp.zeros((8, half), jnp.float32)
    for i, row in enumerate(rows):
        tile = jnp.where(line == i, jnp.broadcast_to(row, (8, half)), tile)
    return tile


def affine(tile, count, gain, shift):
    mean = lane_groups(tile) * (1.0 / GROUP)
    off = tile - mean
    inner = pltpu.roll(off * off * count, 2, 0)
    variance = lane_groups(tile + inner) * (1.0 / (GROUP * count))
    mean = jnp.concatenate([mean[0:1], mean[1:2]], 1)
    variance = jnp.concatenate([variance[2:3], variance[3:4]], 1)
    return mean, 0.5 * gain / jnp.sqrt(variance + EPS), 0.5 * shift


def activated(raw, norm):
    mean, scale, shift = norm
    half = (raw.astype(jnp.float32) - mean) * scale + shift
    return half + half * jnp.tanh(half)


def folded(value):
    cells, chans = value.shape
    return jnp.sum(value.reshape(cells // 8, 8, chans), 0)


def joined(wide, rows, columns, chans):
    wide = wide.reshape(rows, columns, 3 * chans)
    column = lax.broadcasted_iota(jnp.int32, (rows, columns, chans), 1)
    left = jnp.where(column == 0, 0.0, pltpu.roll(wide[:, :, :chans], 1, 1))
    right = jnp.where(
        column == columns - 1, 0.0, pltpu.roll(wide[:, :, 2 * chans :], columns - 1, 1)
    )
    return left + wide[:, :, chans : 2 * chans] + right


def products(field, weight, layer, taps, row, rows):
    columns, chans = field.shape[2:]
    left = [
        field[frame, row + dh : row + dh + rows].reshape(rows * columns, chans)
        for _, frame in taps
        for dh in range(3)
    ]
    right = [weight[layer, dt].reshape(3 * chans, 3 * chans) for dt, _ in taps]
    wide = jnp.dot(
        jnp.concatenate(left, 1),
        jnp.concatenate(right, 0),
        preferred_element_type=jnp.float32,
    )
    return joined(wide, rows, columns, chans)


def kernel(
    frames_all, lines_all,
    features, weights, bias, gain, shift, out,
    raw0, raw1, act0, act1, weight, total, space_stats, tm_stats, pivot,
    in_sem, weight_sem,
    halo_send, halo_recv, edge_send, edge_recv, far_send, far_recv, stat_send, stat_recv,
):
    t, s = lax.axis_index("tm"), lax.axis_index("space")
    later, above, below = lax.rem(t + 1, frames_all), lax.rem(s + lines_all - 1, lines_all), lax.rem(s + 1, lines_all)
    frames, rows, columns, chans = out.shape
    cells = frames * rows * columns
    first = t == 0
    raws, acts = (raw0, raw1), (act0, act1)

    barrier = pltpu.get_barrier_semaphore()

    @pl.loop(1, lines_all)
    def _(j):
        pl.semaphore_signal(barrier, inc=1, device_id=(t, lax.rem(s + j, lines_all)), device_id_type=pl.DeviceIdType.MESH)

    @pl.loop(1, frames_all)
    def _(j):
        pl.semaphore_signal(barrier, inc=1, device_id=(lax.rem(t + j, frames_all), s), device_id_type=pl.DeviceIdType.MESH)

    load = pltpu.make_async_copy(features, raw0.at[pl.ds(2, frames), pl.ds(1, rows)], in_sem)
    load.start()
    loads = []
    for layer in range(2):
        for dw in range(3):
            loads.append(
                pltpu.make_async_copy(
                    weights.at[layer, :, :, dw],
                    weight.at[layer, :, :, :, pl.ds(dw * chans, chans)],
                    weight_sem.at[layer, dw],
                )
            )
            loads[-1].start()

    def remote(source, target, send, recv, device):
        return pltpu.make_async_remote_copy(
            src_ref=source, dst_ref=target, send_sem=send, recv_sem=recv,
            device_id=device, device_id_type=pl.DeviceIdType.MESH,
        )

    def halo(layer, order, k):
        row, count = order[k]
        raw = raws[layer]
        return remote(
            raw.at[pl.ds(2, 2), pl.ds(1 + row, count)],
            raw.at[pl.ds(0, 2), pl.ds(1 + row, count)],
            halo_send.at[layer, k], halo_recv.at[layer, k], (later, s),
        )

    def edge(layer, frame, side, sems):
        raw = raws[layer]
        source, target = ((1, rows + 1), (rows, 0))[side]
        return remote(
            raw.at[pl.ds(frame, 2), source], raw.at[pl.ds(frame, 2), target],
            sems[0].at[layer, side], sems[1].at[layer, side], (t, (above, below)[side]),
        )

    def own_edge(layer, side):
        return edge(layer, 2, side, (edge_send, edge_recv))

    def far_edge(layer, side):
        return edge(layer, 0, side, (far_send, far_recv))

    def spread_start(layer, stage):
        buffer = (space_stats, tm_stats)[stage]
        number = buffer.shape[1]

        @pl.loop(0, number - 1)
        def _(i):
            j = lax.rem(i + number // 3, number - 1) + 1
            device = ((t, lax.rem(s + j, lines_all)), (lax.rem(t + j, frames_all), s))[stage]
            remote(
                buffer.at[layer, 0, pl.ds(0, 4)], buffer.at[layer, j, pl.ds(0, 4)],
                stat_send.at[layer, stage], stat_recv.at[layer, stage], device,
            ).start()

    def spread_wait(layer, stage, sems):
        buffer = (space_stats, tm_stats)[stage]
        rest = buffer.at[layer, pl.ds(1, buffer.shape[1] - 1), pl.ds(0, 4)]
        pltpu.make_async_copy(rest, rest, sems.at[layer, stage]).wait()

    def normalize(layer, norm, frame, row, count):
        raw, act = raws[layer], acts[layer]
        value = raw[frame, pl.ds(row, count)]
        if isinstance(frame, int) and frame < 2:
            value = jnp.where(first, raw[2, pl.ds(row, count)], value)
        value = activated(value, norm)
        if isinstance(row, int) and row in (0, rows + 1):
            outside = s == (0 if row == 0 else lines_all - 1)
            value = jnp.where(outside, 0.0, value)
        act[frame, pl.ds(row, count)] = value.astype(jnp.bfloat16)

    def own_part(layer, norm):
        for side in range(2):
            own_edge(layer, side).wait_recv()
        for dw in range(3):
            loads[3 * layer + dw].wait()
        act = acts[layer]
        half = rows // 2
        added = bias[layer : layer + 1]
        for frame in (2, 3):
            normalize(layer, norm, frame, 0, 1)

            @pl.loop(0, half + 1)
            def _(row):
                normalize(layer, norm, frame, row + 1, 1)

        total[0, :half] = products(act, weight, layer, ((2, 2),), 0, half) + added
        normalize(layer, norm, 2, half + 2, half - 1)
        normalize(layer, norm, 2, rows + 1, 1)
        total[1, :half] = products(act, weight, layer, ((1, 2), (2, 3)), 0, half) + added
        normalize(layer, norm, 3, half + 2, half - 1)
        normalize(layer, norm, 3, rows + 1, 1)
        total[0, half:] = products(act, weight, layer, ((2, 2),), half, half) + added
        total[1, half:] = products(act, weight, layer, ((1, 2), (2, 3)), half, half) + added

    def halo_part(layer, norm, steps, order, finish):
        act = acts[layer]
        done = 0
        ready = -1
        for k, (row, count, need) in enumerate(steps):
            for c in range(done, need + 1):
                if order[c][0] not in (0, rows - 1):
                    halo(layer, order, c).wait_recv()
            done = need + 1
            if k == 0:
                far_edge(layer, 1).wait_recv()
                for frame in (0, 1):
                    normalize(layer, norm, frame, 0, 1)
            if k == len(steps) - 1:
                far_edge(layer, 0).wait_recv()
                for frame in (0, 1):
                    normalize(layer, norm, frame, rows + 1, 1)
            upto = min(row + count, rows - 1)
            for frame in (0, 1):
                normalize(layer, norm, frame, ready + 2, upto - ready)
            ready = upto
            values = (
                products(act, weight, layer, ((0, 0), (1, 1)), row, count),
                products(act, weight, layer, ((0, 1),), row, count),
            )
            finish(k, row, count, values)

    load.wait()

    base = jnp.sum(folded(raw0[2, 1].astype(jnp.float32)), 0, keepdims=True) * (1.0 / columns)

    def line(i, carry):
        sums = list(carry)
        for frame in range(frames):
            off = raw0[2 + frame, 1 + i].astype(jnp.float32) - base
            sums[0] = sums[0] + folded(off)
            sums[1] = sums[1] + folded(off * off)
        return tuple(sums)

    empty = jnp.zeros((8, chans), jnp.float32)
    sums = [jnp.sum(part, 0, keepdims=True) for part in lax.fori_loop(0, rows, line, (empty, empty))]
    off_mean = sums[0] * (1.0 / cells)
    mean, squares = base + off_mean, sums[1] - off_mean * off_mean * cells
    space_stats[0, 0] = packed(mean, squares)

    pl.semaphore_wait(barrier, lines_all + frames_all - 2)

    for k in range(AHEAD[0]):
        halo(0, HALO_0, k).start()
    spread_start(0, 0)
    for side in range(2):
        own_edge(0, side).start()

    def statistics(layer, order, between):
        spread_wait(layer, 0, stat_recv)
        tm_stats[layer, 0] = merged(space_stats[layer], float(cells))
        spread_start(layer, 1)
        for k in range(AHEAD[layer], len(order)):
            halo(layer, order, k).start()
        between()
        spread_wait(layer, 1, stat_recv)
        tile = merged(tm_stats[layer], float(cells * lines_all))
        return affine(
            tile, float(cells * lines_all * frames_all),
            gain[layer : layer + 1], shift[layer : layer + 1],
        )

    def forward_edges(layer, order):
        for k, (row, _) in enumerate(order):
            if row in (0, rows - 1):
                halo(layer, order, k).wait_recv()
                far_edge(layer, 0 if row == 0 else 1).start()

    norm0 = statistics(0, HALO_0, lambda: forward_edges(0, HALO_0))
    own_part(0, norm0)

    sums = [jnp.zeros((8, chans), jnp.float32), jnp.zeros((8, chans), jnp.float32)]

    def finish_0(k, row, count, values):
        chunk = []
        for frame in range(2):
            value = (total[frame, row : row + count] + values[frame]).astype(jnp.bfloat16)
            raw1[2 + frame, 1 + row : 1 + row + count] = value
            chunk.append(value.astype(jnp.float32).reshape(count * columns, chans))
        if k == 0:
            pivot[...] = jnp.sum(folded(chunk[0]) + folded(chunk[1]), 0, keepdims=True) * (
                1.0 / (2 * count * columns)
            )
        base = pivot[...]
        for value in chunk:
            off = value - base
            sums[0] = sums[0] + folded(off)
            sums[1] = sums[1] + folded(off * off)
        if k == 0:
            own_edge(1, 0).start()
        for c in range(AHEAD[1]):
            last = sum(HALO_1[c]) - 1
            if row <= last < row + count:
                halo(1, HALO_1, c).start()

    halo_part(0, norm0, STEPS_0, HALO_0, finish_0)

    off_mean = jnp.sum(sums[0], 0, keepdims=True) * (1.0 / cells)
    off_squares = jnp.sum(sums[1], 0, keepdims=True)
    space_stats[1, 0] = packed(pivot[...] + off_mean, off_squares - off_mean * off_mean * cells)
    spread_start(1, 0)
    own_edge(1, 1).start()
    norm1 = statistics(1, HALO_1, lambda: forward_edges(1, HALO_1))
    own_part(1, norm1)

    def finish_1(k, row, count, values):
        for frame in range(2):
            value = total[frame, row : row + count] + values[frame]
            value = value + raw0[2 + frame, 1 + row : 1 + row + count].astype(jnp.float32)
            out[frame, row : row + count] = value.astype(jnp.bfloat16)

    halo_part(1, norm1, STEPS_1, HALO_1, finish_1)

    for layer in range(2):
        for stage in range(2):
            spread_wait(layer, stage, stat_send)
        for side in range(2):
            own_edge(layer, side).wait_send()
            far_edge(layer, side).wait_send()
    for k in range(len(HALO_0)):
        halo(0, HALO_0, k).wait_send()
    for k in range(len(HALO_1)):
        halo(1, HALO_1, k).wait_send()


def shards(features, weights, bias, gain, shift):
    frames, rows, columns, chans = features.shape
    frames_all, lines_all = lax.axis_size("tm"), lax.axis_size("space")
    field = pltpu.VMEM((frames + 2, rows + 2, columns, chans), jnp.bfloat16)
    there, here = pl.BlockSpec(memory_space=pltpu.HBM), pl.BlockSpec(memory_space=pltpu.VMEM)
    return pl.pallas_call(
        functools.partial(kernel, frames_all, lines_all),
        out_shape=pltpu.VMEM(features.shape, features.dtype),
        in_specs=[there, there, here, here, here],
        out_specs=here,
        scratch_shapes=[
            field, field, field, field,
            pltpu.VMEM((2, 3, 3, chans, 3 * chans), jnp.bfloat16),
            pltpu.VMEM((frames, rows, columns, chans), jnp.float32),
            pltpu.VMEM((2, lines_all, 8, 128), jnp.float32),
            pltpu.VMEM((2, frames_all, 8, 128), jnp.float32),
            pltpu.VMEM((1, chans), jnp.float32),
            DMA, DMA((2, 3)),
            DMA((2, 8)), DMA((2, 8)),
            DMA((2, 2)), DMA((2, 2)), DMA((2, 2)), DMA((2, 2)),
            DMA((2, 2)), DMA((2, 2)),
        ],
        compiler_params=pltpu.CompilerParams(
            collective_id=0, has_side_effects=True, vmem_limit_bytes=56 * 2**20
        ),
        cost_estimate=pl.CostEstimate(
            flops=4 * frames * rows * columns * 27 * chans * chans,
            bytes_accessed=2 * features.size * 2 + weights.size * 2,
            transcendentals=0,
        ),
    )(features, weights, bias, gain, shift)


def solution(mesh):
    placed = (P("tm", "space", None, None), P(), P(), P(), P())
    return jax.shard_map(
        shards, mesh=mesh, in_specs=placed, out_specs=P("tm", "space", None, None), check_vma=False
    )
```

```python
import functools

import jax
import jax.numpy as jnp
from jax import lax
from jax.experimental import pallas as pl
from jax.experimental.pallas import tpu as pltpu
from jax.sharding import PartitionSpec as P

GROUP = 8
EPS = 1e-06
DMA = pltpu.SemaphoreType.DMA

HALO_0 = ((0, 1), (7, 1), (1, 1), (2, 2), (4, 2), (6, 1))
HALO_1 = ((0, 1), (1, 2), (3, 1), (4, 1), (7, 1), (5, 1), (6, 1))
AHEAD = (3, 4)
STEPS_0 = ((0, 3, 3), (3, 2, 4), (5, 3, 5))
STEPS_1 = ((0, 3, 2), (3, 2, 5), (5, 3, 6))


def lane_groups(tile):
    lanes = tile.shape[1]
    lane = lax.broadcasted_iota(jnp.int32, tile.shape, 1)
    step = 1
    while step < GROUP:
        ahead = pltpu.roll(tile, lanes - step, 1)
        behind = pltpu.roll(tile, step, 1)
        tile = tile + jnp.where(lane % (2 * step) < step, ahead, behind)
        step *= 2
    return tile


def merged(parts, each):
    total = jnp.sum(parts, 0)
    mean = total * (1.0 / parts.shape[0])
    off = parts - mean
    spread = jnp.sum(off * off, 0) * each
    shifted = pltpu.roll(spread, 2, 0)
    line = lax.broadcasted_iota(jnp.int32, total.shape, 0)
    return jnp.where(line < 2, mean, total + shifted)


def packed(mean, squares):
    half = mean.shape[1] // 2
    line = lax.broadcasted_iota(jnp.int32, (8, half), 0)
    rows = (mean[:, :half], mean[:, half:], squares[:, :half], squares[:, half:])
    tile = jnp.zeros((8, half), jnp.float32)
    for i, row in enumerate(rows):
        tile = jnp.where(line == i, jnp.broadcast_to(row, (8, half)), tile)
    return tile


def affine(tile, count, gain, shift):
    mean = lane_groups(tile) * (1.0 / GROUP)
    off = tile - mean
    inner = pltpu.roll(off * off * count, 2, 0)
    variance = lane_groups(tile + inner) * (1.0 / (GROUP * count))
    mean = jnp.concatenate([mean[0:1], mean[1:2]], 1)
    variance = jnp.concatenate([variance[2:3], variance[3:4]], 1)
    return mean, 0.5 * gain / jnp.sqrt(variance + EPS), 0.5 * shift


def activated(raw, norm):
    mean, scale, shift = norm
    half = (raw.astype(jnp.float32) - mean) * scale + shift
    return half + half * jnp.tanh(half)


def folded(value):
    cells, chans = value.shape
    return jnp.sum(value.reshape(cells // 8, 8, chans), 0)


def joined(wide, rows, columns, chans):
    wide = wide.reshape(rows, columns, 3 * chans)
    column = lax.broadcasted_iota(jnp.int32, (rows, columns, chans), 1)
    left = jnp.where(column == 0, 0.0, pltpu.roll(wide[:, :, :chans], 1, 1))
    right = jnp.where(
        column == columns - 1, 0.0, pltpu.roll(wide[:, :, 2 * chans :], columns - 1, 1)
    )
    return left + wide[:, :, chans : 2 * chans] + right


def products(field, weight, layer, taps, row, rows):
    columns, chans = field.shape[2:]
    left = [
        field[frame, row + dh : row + dh + rows].reshape(rows * columns, chans)
        for _, frame in taps
        for dh in range(3)
    ]
    right = [weight[layer, dt].reshape(3 * chans, 3 * chans) for dt, _ in taps]
    wide = jnp.dot(
        jnp.concatenate(left, 1),
        jnp.concatenate(right, 0),
        preferred_element_type=jnp.float32,
    )
    return joined(wide, rows, columns, chans)


def kernel(
    frames_all, lines_all,
    features, weights, bias, gain, shift, out,
    raw0, raw1, act0, act1, weight, total, space_stats, tm_stats, pivot,
    in_sem, weight_sem,
    halo_send, halo_recv, edge_send, edge_recv, far_send, far_recv, stat_send, stat_recv,
):
    t, s = lax.axis_index("tm"), lax.axis_index("space")
    later, above, below = lax.rem(t + 1, frames_all), lax.rem(s + lines_all - 1, lines_all), lax.rem(s + 1, lines_all)
    frames, rows, columns, chans = out.shape
    cells = frames * rows * columns
    first = t == 0
    raws, acts = (raw0, raw1), (act0, act1)

    barrier = pltpu.get_barrier_semaphore()

    @pl.loop(1, lines_all)
    def _(j):
        pl.semaphore_signal(barrier, inc=1, device_id=(t, lax.rem(s + j, lines_all)), device_id_type=pl.DeviceIdType.MESH)

    @pl.loop(1, frames_all)
    def _(j):
        pl.semaphore_signal(barrier, inc=1, device_id=(lax.rem(t + j, frames_all), s), device_id_type=pl.DeviceIdType.MESH)

    load = pltpu.make_async_copy(features, raw0.at[pl.ds(2, frames), pl.ds(1, rows)], in_sem)
    load.start()
    loads = []
    for layer in range(2):
        for dw in range(3):
            loads.append(
                pltpu.make_async_copy(
                    weights.at[layer, :, :, dw],
                    weight.at[layer, :, :, :, pl.ds(dw * chans, chans)],
                    weight_sem.at[layer, dw],
                )
            )
            loads[-1].start()

    def remote(source, target, send, recv, device):
        return pltpu.make_async_remote_copy(
            src_ref=source, dst_ref=target, send_sem=send, recv_sem=recv,
            device_id=device, device_id_type=pl.DeviceIdType.MESH,
        )

    def halo(layer, order, k):
        row, count = order[k]
        raw = raws[layer]
        return remote(
            raw.at[pl.ds(2, 2), pl.ds(1 + row, count)],
            raw.at[pl.ds(0, 2), pl.ds(1 + row, count)],
            halo_send.at[layer, k], halo_recv.at[layer, k], (later, s),
        )

    def edge(layer, frame, side, sems):
        raw = raws[layer]
        source, target = ((1, rows + 1), (rows, 0))[side]
        return remote(
            raw.at[pl.ds(frame, 2), source], raw.at[pl.ds(frame, 2), target],
            sems[0].at[layer, side], sems[1].at[layer, side], (t, (above, below)[side]),
        )

    def own_edge(layer, side):
        return edge(layer, 2, side, (edge_send, edge_recv))

    def far_edge(layer, side):
        return edge(layer, 0, side, (far_send, far_recv))

    def spread_start(layer, stage):
        buffer = (space_stats, tm_stats)[stage]
        number = buffer.shape[1]

        @pl.loop(0, number - 1)
        def _(i):
            j = lax.rem(i + number // 3, number - 1) + 1
            device = ((t, lax.rem(s + j, lines_all)), (lax.rem(t + j, frames_all), s))[stage]
            remote(
                buffer.at[layer, 0, pl.ds(0, 4)], buffer.at[layer, j, pl.ds(0, 4)],
                stat_send.at[layer, stage], stat_recv.at[layer, stage], device,
            ).start()

    def spread_wait(layer, stage, sems):
        buffer = (space_stats, tm_stats)[stage]
        rest = buffer.at[layer, pl.ds(1, buffer.shape[1] - 1), pl.ds(0, 4)]
        pltpu.make_async_copy(rest, rest, sems.at[layer, stage]).wait()

    def normalize(layer, norm, frame, row, count):
        raw, act = raws[layer], acts[layer]
        value = raw[frame, pl.ds(row, count)]
        if isinstance(frame, int) and frame < 2:
            value = jnp.where(first, raw[2, pl.ds(row, count)], value)
        value = activated(value, norm)
        if isinstance(row, int) and row in (0, rows + 1):
            outside = s == (0 if row == 0 else lines_all - 1)
            value = jnp.where(outside, 0.0, value)
        act[frame, pl.ds(row, count)] = value.astype(jnp.bfloat16)

    def own_part(layer, norm):
        for side in range(2):
            own_edge(layer, side).wait_recv()
        for dw in range(3):
            loads[3 * layer + dw].wait()
        act = acts[layer]
        half = rows // 2
        added = bias[layer : layer + 1]
        for frame in (2, 3):
            normalize(layer, norm, frame, 0, 1)

            @pl.loop(0, half + 1)
            def _(row):
                normalize(layer, norm, frame, row + 1, 1)

        total[0, :half] = products(act, weight, layer, ((2, 2),), 0, half) + added
        normalize(layer, norm, 2, half + 2, half - 1)
        normalize(layer, norm, 2, rows + 1, 1)
        total[1, :half] = products(act, weight, layer, ((1, 2), (2, 3)), 0, half) + added
        normalize(layer, norm, 3, half + 2, half - 1)
        normalize(layer, norm, 3, rows + 1, 1)
        total[0, half:] = products(act, weight, layer, ((2, 2),), half, half) + added
        total[1, half:] = products(act, weight, layer, ((1, 2), (2, 3)), half, half) + added

    def halo_part(layer, norm, steps, order, finish):
        act = acts[layer]
        done = 0
        ready = -1
        for k, (row, count, need) in enumerate(steps):
            for c in range(done, need + 1):
                if order[c][0] not in (0, rows - 1):
                    halo(layer, order, c).wait_recv()
            done = need + 1
            if k == 0:
                far_edge(layer, 1).wait_recv()
                for frame in (0, 1):
                    normalize(layer, norm, frame, 0, 1)
            if k == len(steps) - 1:
                far_edge(layer, 0).wait_recv()
                for frame in (0, 1):
                    normalize(layer, norm, frame, rows + 1, 1)
            upto = min(row + count, rows - 1)
            for frame in (0, 1):
                normalize(layer, norm, frame, ready + 2, upto - ready)
            ready = upto
            values = (
                products(act, weight, layer, ((0, 0), (1, 1)), row, count),
                products(act, weight, layer, ((0, 1),), row, count),
            )
            finish(k, row, count, values)

    load.wait()

    base = jnp.sum(folded(raw0[2, 1].astype(jnp.float32)), 0, keepdims=True) * (1.0 / columns)

    def line(i, carry):
        sums = list(carry)
        for frame in range(frames):
            off = raw0[2 + frame, 1 + i].astype(jnp.float32) - base
            sums[0] = sums[0] + folded(off)
            sums[1] = sums[1] + folded(off * off)
        return tuple(sums)

    empty = jnp.zeros((8, chans), jnp.float32)
    sums = [jnp.sum(part, 0, keepdims=True) for part in lax.fori_loop(0, rows, line, (empty, empty))]
    off_mean = sums[0] * (1.0 / cells)
    mean, squares = base + off_mean, sums[1] - off_mean * off_mean * cells
    space_stats[0, 0] = packed(mean, squares)

    pl.semaphore_wait(barrier, lines_all + frames_all - 2)

    for k in range(AHEAD[0]):
        halo(0, HALO_0, k).start()
    spread_start(0, 0)
    for side in range(2):
        own_edge(0, side).start()

    def statistics(layer, order, between):
        spread_wait(layer, 0, stat_recv)
        tm_stats[layer, 0] = merged(space_stats[layer], float(cells))
        spread_start(layer, 1)
        for k in range(AHEAD[layer], len(order)):
            halo(layer, order, k).start()
        between()
        spread_wait(layer, 1, stat_recv)
        tile = merged(tm_stats[layer], float(cells * lines_all))
        return affine(
            tile, float(cells * lines_all * frames_all),
            gain[layer : layer + 1], shift[layer : layer + 1],
        )

    def forward_edges(layer, order):
        for k, (row, _) in enumerate(order):
            if row in (0, rows - 1):
                halo(layer, order, k).wait_recv()
                far_edge(layer, 0 if row == 0 else 1).start()

    norm0 = statistics(0, HALO_0, lambda: forward_edges(0, HALO_0))
    own_part(0, norm0)

    sums = [jnp.zeros((8, chans), jnp.float32), jnp.zeros((8, chans), jnp.float32)]

    def finish_0(k, row, count, values):
        chunk = []
        for frame in range(2):
            value = (total[frame, row : row + count] + values[frame]).astype(jnp.bfloat16)
            raw1[2 + frame, 1 + row : 1 + row + count] = value
            chunk.append(value.astype(jnp.float32).reshape(count * columns, chans))
        if k == 0:
            pivot[...] = jnp.sum(folded(chunk[0]) + folded(chunk[1]), 0, keepdims=True) * (
                1.0 / (2 * count * columns)
            )
        base = pivot[...]
        for value in chunk:
            off = value - base
            sums[0] = sums[0] + folded(off)
            sums[1] = sums[1] + folded(off * off)
        if k == 0:
            own_edge(1, 0).start()
        for c in range(AHEAD[1]):
            last = sum(HALO_1[c]) - 1
            if row <= last < row + count:
                halo(1, HALO_1, c).start()

    halo_part(0, norm0, STEPS_0, HALO_0, finish_0)

    off_mean = jnp.sum(sums[0], 0, keepdims=True) * (1.0 / cells)
    off_squares = jnp.sum(sums[1], 0, keepdims=True)
    space_stats[1, 0] = packed(pivot[...] + off_mean, off_squares - off_mean * off_mean * cells)
    spread_start(1, 0)
    own_edge(1, 1).start()
    norm1 = statistics(1, HALO_1, lambda: forward_edges(1, HALO_1))
    own_part(1, norm1)

    def finish_1(k, row, count, values):
        for frame in range(2):
            value = total[frame, row : row + count] + values[frame]
            value = value + raw0[2 + frame, 1 + row : 1 + row + count].astype(jnp.float32)
            out[frame, row : row + count] = value.astype(jnp.bfloat16)

    halo_part(1, norm1, STEPS_1, HALO_1, finish_1)

    for layer in range(2):
        for stage in range(2):
            spread_wait(layer, stage, stat_send)
        for side in range(2):
            own_edge(layer, side).wait_send()
            far_edge(layer, side).wait_send()
    for k in range(len(HALO_0)):
        halo(0, HALO_0, k).wait_send()
    for k in range(len(HALO_1)):
        halo(1, HALO_1, k).wait_send()


def shards(features, weights, bias, gain, shift):
    frames, rows, columns, chans = features.shape
    frames_all, lines_all = lax.axis_size("tm"), lax.axis_size("space")
    field = pltpu.VMEM((frames + 2, rows + 2, columns, chans), jnp.bfloat16)
    there, here = pl.BlockSpec(memory_space=pltpu.HBM), pl.BlockSpec(memory_space=pltpu.VMEM)
    return pl.pallas_call(
        functools.partial(kernel, frames_all, lines_all),
        out_shape=pltpu.VMEM(features.shape, features.dtype),
        in_specs=[there, there, here, here, here],
        out_specs=here,
        scratch_shapes=[
            field, field, field, field,
            pltpu.VMEM((2, 3, 3, chans, 3 * chans), jnp.bfloat16),
            pltpu.VMEM((frames, rows, columns, chans), jnp.float32),
            pltpu.VMEM((2, lines_all, 8, 128), jnp.float32),
            pltpu.VMEM((2, frames_all, 8, 128), jnp.float32),
            pltpu.VMEM((1, chans), jnp.float32),
            DMA, DMA((2, 3)),
            DMA((2, 8)), DMA((2, 8)),
            DMA((2, 2)), DMA((2, 2)), DMA((2, 2)), DMA((2, 2)),
            DMA((2, 2)), DMA((2, 2)),
        ],
        compiler_params=pltpu.CompilerParams(
            collective_id=0, has_side_effects=True, vmem_limit_bytes=56 * 2**20
        ),
        cost_estimate=pl.CostEstimate(
            flops=4 * frames * rows * columns * 27 * chans * chans,
            bytes_accessed=2 * features.size * 2 + weights.size * 2,
            transcendentals=0,
        ),
    )(features, weights, bias, gain, shift)


def solution(mesh):
    placed = (P("tm", "space", None, None), P(), P(), P(), P())
    return jax.shard_map(
        shards, mesh=mesh, in_specs=placed, out_specs=P("tm", "space", None, None), check_vma=False
    )
```

```python
import functools

import jax
import jax.numpy as jnp
from jax import lax
from jax.experimental import pallas as pl
from jax.experimental.pallas import tpu as pltpu
from jax.sharding import PartitionSpec as P

GROUP = 8
EPS = 1e-06
DMA = pltpu.SemaphoreType.DMA

HALO_0 = ((0, 1), (7, 1), (1, 1), (2, 2), (4, 2), (6, 1))
HALO_1 = ((0, 1), (1, 2), (3, 1), (4, 1), (7, 1), (5, 1), (6, 1))
AHEAD = (3, 4)
STEPS_0 = ((0, 3, 3), (3, 2, 4), (5, 3, 5))
STEPS_1 = ((0, 3, 2), (3, 2, 5), (5, 3, 6))


def lane_groups(tile):
    lanes = tile.shape[1]
    lane = lax.broadcasted_iota(jnp.int32, tile.shape, 1)
    step = 1
    while step < GROUP:
        ahead = pltpu.roll(tile, lanes - step, 1)
        behind = pltpu.roll(tile, step, 1)
        tile = tile + jnp.where(lane % (2 * step) < step, ahead, behind)
        step *= 2
    return tile


def merged(parts, each):
    total = jnp.sum(parts, 0)
    mean = total * (1.0 / parts.shape[0])
    off = parts - mean
    spread = jnp.sum(off * off, 0) * each
    shifted = pltpu.roll(spread, 2, 0)
    line = lax.broadcasted_iota(jnp.int32, total.shape, 0)
    return jnp.where(line < 2, mean, total + shifted)


def packed(mean, squares):
    half = mean.shape[1] // 2
    line = lax.broadcasted_iota(jnp.int32, (8, half), 0)
    rows = (mean[:, :half], mean[:, half:], squares[:, :half], squares[:, half:])
    tile = jnp.zeros((8, half), jnp.float32)
    for i, row in enumerate(rows):
        tile = jnp.where(line == i, jnp.broadcast_to(row, (8, half)), tile)
    return tile


def affine(tile, count, gain, shift):
    mean = lane_groups(tile) * (1.0 / GROUP)
    off = tile - mean
    inner = pltpu.roll(off * off * count, 2, 0)
    variance = lane_groups(tile + inner) * (1.0 / (GROUP * count))
    mean = jnp.concatenate([mean[0:1], mean[1:2]], 1)
    variance = jnp.concatenate([variance[2:3], variance[3:4]], 1)
    return mean, 0.5 * gain / jnp.sqrt(variance + EPS), 0.5 * shift


def activated(raw, norm):
    mean, scale, shift = norm
    half = (raw.astype(jnp.float32) - mean) * scale + shift
    return half + half * jnp.tanh(half)


def folded(value):
    cells, chans = value.shape
    return jnp.sum(value.reshape(cells // 8, 8, chans), 0)


def joined(wide, rows, columns, chans):
    wide = wide.reshape(rows, columns, 3 * chans)
    column = lax.broadcasted_iota(jnp.int32, (rows, columns, chans), 1)
    left = jnp.where(column == 0, 0.0, pltpu.roll(wide[:, :, :chans], 1, 1))
    right = jnp.where(
        column == columns - 1, 0.0, pltpu.roll(wide[:, :, 2 * chans :], columns - 1, 1)
    )
    return left + wide[:, :, chans : 2 * chans] + right


def products(field, weight, layer, taps, row, rows):
    columns, chans = field.shape[2:]
    left = [
        field[frame, row + dh : row + dh + rows].reshape(rows * columns, chans)
        for _, frame in taps
        for dh in range(3)
    ]
    right = [weight[layer, dt].reshape(3 * chans, 3 * chans) for dt, _ in taps]
    wide = jnp.dot(
        jnp.concatenate(left, 1),
        jnp.concatenate(right, 0),
        preferred_element_type=jnp.float32,
    )
    return joined(wide, rows, columns, chans)


def kernel(
    frames_all, lines_all,
    features, weights, bias, gain, shift, out,
    raw0, raw1, act0, act1, weight, total, space_stats, tm_stats, pivot,
    in_sem, weight_sem,
    halo_send, halo_recv, edge_send, edge_recv, far_send, far_recv, stat_send, stat_recv,
):
    t, s = lax.axis_index("tm"), lax.axis_index("space")
    later, above, below = lax.rem(t + 1, frames_all), lax.rem(s + lines_all - 1, lines_all), lax.rem(s + 1, lines_all)
    frames, rows, columns, chans = out.shape
    cells = frames * rows * columns
    first = t == 0
    raws, acts = (raw0, raw1), (act0, act1)

    barrier = pltpu.get_barrier_semaphore()

    @pl.loop(1, lines_all)
    def _(j):
        pl.semaphore_signal(barrier, inc=1, device_id=(t, lax.rem(s + j, lines_all)), device_id_type=pl.DeviceIdType.MESH)

    @pl.loop(1, frames_all)
    def _(j):
        pl.semaphore_signal(barrier, inc=1, device_id=(lax.rem(t + j, frames_all), s), device_id_type=pl.DeviceIdType.MESH)

    load = pltpu.make_async_copy(features, raw0.at[pl.ds(2, frames), pl.ds(1, rows)], in_sem)
    load.start()
    loads = []
    for layer in range(2):
        for dw in range(3):
            loads.append(
                pltpu.make_async_copy(
                    weights.at[layer, :, :, dw],
                    weight.at[layer, :, :, :, pl.ds(dw * chans, chans)],
                    weight_sem.at[layer, dw],
                )
            )
            loads[-1].start()

    def remote(source, target, send, recv, device):
        return pltpu.make_async_remote_copy(
            src_ref=source, dst_ref=target, send_sem=send, recv_sem=recv,
            device_id=device, device_id_type=pl.DeviceIdType.MESH,
        )

    def halo(layer, order, k):
        row, count = order[k]
        raw = raws[layer]
        return remote(
            raw.at[pl.ds(2, 2), pl.ds(1 + row, count)],
            raw.at[pl.ds(0, 2), pl.ds(1 + row, count)],
            halo_send.at[layer, k], halo_recv.at[layer, k], (later, s),
        )

    def edge(layer, frame, side, sems):
        raw = raws[layer]
        source, target = ((1, rows + 1), (rows, 0))[side]
        return remote(
            raw.at[pl.ds(frame, 2), source], raw.at[pl.ds(frame, 2), target],
            sems[0].at[layer, side], sems[1].at[layer, side], (t, (above, below)[side]),
        )

    def own_edge(layer, side):
        return edge(layer, 2, side, (edge_send, edge_recv))

    def far_edge(layer, side):
        return edge(layer, 0, side, (far_send, far_recv))

    def spread_start(layer, stage):
        buffer = (space_stats, tm_stats)[stage]
        number = buffer.shape[1]

        @pl.loop(0, number - 1)
        def _(i):
            j = lax.rem(i + number // 3, number - 1) + 1
            device = ((t, lax.rem(s + j, lines_all)), (lax.rem(t + j, frames_all), s))[stage]
            remote(
                buffer.at[layer, 0, pl.ds(0, 4)], buffer.at[layer, j, pl.ds(0, 4)],
                stat_send.at[layer, stage], stat_recv.at[layer, stage], device,
            ).start()

    def spread_wait(layer, stage, sems):
        buffer = (space_stats, tm_stats)[stage]
        rest = buffer.at[layer, pl.ds(1, buffer.shape[1] - 1), pl.ds(0, 4)]
        pltpu.make_async_copy(rest, rest, sems.at[layer, stage]).wait()

    def normalize(layer, norm, frame, row, count):
        raw, act = raws[layer], acts[layer]
        value = raw[frame, pl.ds(row, count)]
        if isinstance(frame, int) and frame < 2:
            value = jnp.where(first, raw[2, pl.ds(row, count)], value)
        value = activated(value, norm)
        if isinstance(row, int) and row in (0, rows + 1):
            outside = s == (0 if row == 0 else lines_all - 1)
            value = jnp.where(outside, 0.0, value)
        act[frame, pl.ds(row, count)] = value.astype(jnp.bfloat16)

    def own_part(layer, norm):
        for side in range(2):
            own_edge(layer, side).wait_recv()
        for dw in range(3):
            loads[3 * layer + dw].wait()
        act = acts[layer]
        half = rows // 2
        added = bias[layer : layer + 1]
        for frame in (2, 3):
            normalize(layer, norm, frame, 0, 1)

            @pl.loop(0, half + 1)
            def _(row):
                normalize(layer, norm, frame, row + 1, 1)

        total[0, :half] = products(act, weight, layer, ((2, 2),), 0, half) + added
        normalize(layer, norm, 2, half + 2, half - 1)
        normalize(layer, norm, 2, rows + 1, 1)
        total[1, :half] = products(act, weight, layer, ((1, 2), (2, 3)), 0, half) + added
        normalize(layer, norm, 3, half + 2, half - 1)
        normalize(layer, norm, 3, rows + 1, 1)
        if layer == 1:
            for c in (1, 2):
                halo(1, HALO_1, c).wait_recv()
        total[0, half:] = products(act, weight, layer, ((2, 2),), half, half) + added
        if layer == 1:
            normalize(layer, norm, 0, 1, 4)
        total[1, half:] = products(act, weight, layer, ((1, 2), (2, 3)), half, half) + added
        if layer == 1:
            normalize(layer, norm, 1, 1, 4)

    def halo_part(layer, norm, steps, order, finish):
        act = acts[layer]
        done, ready = ((0, -1), (3, 3))[layer]
        for k, (row, count, need) in enumerate(steps):
            for c in range(done, need + 1):
                if order[c][0] not in (0, rows - 1):
                    halo(layer, order, c).wait_recv()
            done = need + 1
            if k == 0:
                far_edge(layer, 1).wait_recv()
                for frame in (0, 1):
                    normalize(layer, norm, frame, 0, 1)
            if k == len(steps) - 1:
                far_edge(layer, 0).wait_recv()
                for frame in (0, 1):
                    normalize(layer, norm, frame, rows + 1, 1)
            upto = min(row + count, rows - 1)
            if upto > ready:
                for frame in (0, 1):
                    normalize(layer, norm, frame, ready + 2, upto - ready)
            ready = upto
            values = (
                products(act, weight, layer, ((0, 0), (1, 1)), row, count),
                products(act, weight, layer, ((0, 1),), row, count),
            )
            finish(k, row, count, values)

    load.wait()

    base = jnp.sum(folded(raw0[2, 1].astype(jnp.float32)), 0, keepdims=True) * (1.0 / columns)

    def line(i, carry):
        sums = list(carry)
        for frame in range(frames):
            off = raw0[2 + frame, 1 + i].astype(jnp.float32) - base
            sums[0] = sums[0] + folded(off)
            sums[1] = sums[1] + folded(off * off)
        return tuple(sums)

    empty = jnp.zeros((8, chans), jnp.float32)
    sums = [jnp.sum(part, 0, keepdims=True) for part in lax.fori_loop(0, rows, line, (empty, empty))]
    off_mean = sums[0] * (1.0 / cells)
    mean, squares = base + off_mean, sums[1] - off_mean * off_mean * cells
    space_stats[0, 0] = packed(mean, squares)

    pl.semaphore_wait(barrier, lines_all + frames_all - 2)

    for k in range(AHEAD[0]):
        halo(0, HALO_0, k).start()
    spread_start(0, 0)
    for side in range(2):
        own_edge(0, side).start()

    def statistics(layer, order, between):
        spread_wait(layer, 0, stat_recv)
        tm_stats[layer, 0] = merged(space_stats[layer], float(cells))
        spread_start(layer, 1)
        for k in range(AHEAD[layer], len(order)):
            halo(layer, order, k).start()
        between()
        spread_wait(layer, 1, stat_recv)
        tile = merged(tm_stats[layer], float(cells * lines_all))
        return affine(
            tile, float(cells * lines_all * frames_all),
            gain[layer : layer + 1], shift[layer : layer + 1],
        )

    def forward_edges(layer, order):
        for k, (row, _) in enumerate(order):
            if row in (0, rows - 1):
                halo(layer, order, k).wait_recv()
                far_edge(layer, 0 if row == 0 else 1).start()

    norm0 = statistics(0, HALO_0, lambda: forward_edges(0, HALO_0))
    own_part(0, norm0)

    sums = [jnp.zeros((8, chans), jnp.float32), jnp.zeros((8, chans), jnp.float32)]

    def finish_0(k, row, count, values):
        chunk = []
        for frame in range(2):
            value = (total[frame, row : row + count] + values[frame]).astype(jnp.bfloat16)
            raw1[2 + frame, 1 + row : 1 + row + count] = value
            chunk.append(value.astype(jnp.float32).reshape(count * columns, chans))
        if k == 0:
            pivot[...] = jnp.sum(folded(chunk[0]) + folded(chunk[1]), 0, keepdims=True) * (
                1.0 / (2 * count * columns)
            )
        base = pivot[...]
        for value in chunk:
            off = value - base
            sums[0] = sums[0] + folded(off)
            sums[1] = sums[1] + folded(off * off)
        if k == 0:
            own_edge(1, 0).start()
        for c in range(AHEAD[1]):
            last = sum(HALO_1[c]) - 1
            if row <= last < row + count:
                halo(1, HALO_1, c).start()

    halo_part(0, norm0, STEPS_0, HALO_0, finish_0)

    off_mean = jnp.sum(sums[0], 0, keepdims=True) * (1.0 / cells)
    off_squares = jnp.sum(sums[1], 0, keepdims=True)
    space_stats[1, 0] = packed(pivot[...] + off_mean, off_squares - off_mean * off_mean * cells)
    spread_start(1, 0)
    own_edge(1, 1).start()
    norm1 = statistics(1, HALO_1, lambda: forward_edges(1, HALO_1))
    own_part(1, norm1)

    def finish_1(k, row, count, values):
        for frame in range(2):
            value = total[frame, row : row + count] + values[frame]
            value = value + raw0[2 + frame, 1 + row : 1 + row + count].astype(jnp.float32)
            out[frame, row : row + count] = value.astype(jnp.bfloat16)

    halo_part(1, norm1, STEPS_1, HALO_1, finish_1)

    for layer in range(2):
        for stage in range(2):
            spread_wait(layer, stage, stat_send)
        for side in range(2):
            own_edge(layer, side).wait_send()
            far_edge(layer, side).wait_send()
    for k in range(len(HALO_0)):
        halo(0, HALO_0, k).wait_send()
    for k in range(len(HALO_1)):
        halo(1, HALO_1, k).wait_send()


def shards(features, weights, bias, gain, shift):
    frames, rows, columns, chans = features.shape
    frames_all, lines_all = lax.axis_size("tm"), lax.axis_size("space")
    field = pltpu.VMEM((frames + 2, rows + 2, columns, chans), jnp.bfloat16)
    there, here = pl.BlockSpec(memory_space=pltpu.HBM), pl.BlockSpec(memory_space=pltpu.VMEM)
    return pl.pallas_call(
        functools.partial(kernel, frames_all, lines_all),
        out_shape=pltpu.VMEM(features.shape, features.dtype),
        in_specs=[there, there, here, here, here],
        out_specs=here,
        scratch_shapes=[
            field, field, field, field,
            pltpu.VMEM((2, 3, 3, chans, 3 * chans), jnp.bfloat16),
            pltpu.VMEM((frames, rows, columns, chans), jnp.float32),
            pltpu.VMEM((2, lines_all, 8, 128), jnp.float32),
            pltpu.VMEM((2, frames_all, 8, 128), jnp.float32),
            pltpu.VMEM((1, chans), jnp.float32),
            DMA, DMA((2, 3)),
            DMA((2, 8)), DMA((2, 8)),
            DMA((2, 2)), DMA((2, 2)), DMA((2, 2)), DMA((2, 2)),
            DMA((2, 2)), DMA((2, 2)),
        ],
        compiler_params=pltpu.CompilerParams(
            collective_id=0, has_side_effects=True, vmem_limit_bytes=56 * 2**20
        ),
        cost_estimate=pl.CostEstimate(
            flops=4 * frames * rows * columns * 27 * chans * chans,
            bytes_accessed=2 * features.size * 2 + weights.size * 2,
            transcendentals=0,
        ),
    )(features, weights, bias, gain, shift)


def solution(mesh):
    placed = (P("tm", "space", None, None), P(), P(), P(), P())
    return jax.shard_map(
        shards, mesh=mesh, in_specs=placed, out_specs=P("tm", "space", None, None), check_vma=False
    )
```
